256 devices in a mesh: gz: 16 (over y, z_hi), gx: 8 (over x, core), gy: 2 (over z_lo).
Axes of the slice: x: 4, y: 4, z: 8 (z_hi: 4, z_lo: 2; z = z_hi * 2 + z_lo), core: 2. Of those that a mesh axis runs over, the one named last changes fastest.
Arguments:
- electric: float32 [3, 256, 128, 256], P(None, 'gz', 'gx', 'gy'), may hold values from -6 to 6
- magnetic: float32 [3, 256, 128, 256], P(None, 'gz', 'gx', 'gy'), may hold values from -6 to 6
- aux_state: float32 [4, 2, 8, 128, 256], P(None, None, None, 'gx', 'gy'), may hold values from -6 to 6
- material: int32 [128, 256], P('gx', 'gy'), may hold values 0 or 1
- kerr_strength: float32 [2], replicated, may hold values from 0.1 to 1
Outputs:
- electric_out: float32 [3, 256, 128, 256], P(None, 'gz', 'gx', 'gy')
- magnetic_out: float32 [3, 256, 128, 256], P(None, 'gz', 'gx', 'gy')
The draws below stay inside these ranges and needn't reach their ends.
Inputs may be any that keep to these rules, and one draw needn't show every extreme that they name: `material`: 0 marks cladding, 1 the waveguide core.
All inputs are finite; a program needn't handle non-finite values. No bound on the sum of `material` on one device may be relied on, other than what follows from the above.
Results may differ from the reference program's by a relative error of at most 0.00002.
Values sent between devices are 32-bit elements; how exact they have to be, the bound alone decides.
No kernel may reach another device: no remote copies, remote signals or barrier semaphores. Data moves between devices by JAX's collectives and lax.ppermute only.
A program may use at most 128 MiB of HBM per device.

```python
import math
import jax
import jax.numpy as jnp

PML = 8
STEPS = 4
NZ = 256
NX = 128
NY = 256


def plant(drawn, rng, least, high):
    longest = drawn.shape.index(max(drawn.shape))
    spots = []
    for shift in (0, 1):
        where = [jax.random.randint(jax.random.fold_in(rng, axis), (), 0, length) for axis, length in enumerate(drawn.shape)]
        where[longest] = (where[longest] + shift) % drawn.shape[longest]
        spots.append(tuple(where))
    return drawn.at[spots[0]].set(least).at[spots[1]].set(high)


def shard_levels(stream_key, shape, split, smallest, high):
    gain, own = 1.0, jax.random.fold_in(stream_key, 6)
    for axis_at, parts in split:
        draws = jnp.exp(jax.random.uniform(jax.random.fold_in(own, axis_at), (parts,), jnp.float32, smallest / len(split), high / len(split)))
        gain = gain * jnp.repeat(draws, shape[axis_at] // parts).reshape([-1 if axis == axis_at else 1 for axis in range(len(shape))])
    return gain


def gaussian(key, shape, deviation, reach, split=(), kind=jnp.bfloat16):
    level = shard_levels(key, shape, split, -0.22, 0.18) if split else 1.0
    entries = jax.random.normal(key, shape, jnp.float32) * deviation * level
    return jnp.minimum(jnp.maximum(entries, -reach), reach).astype(kind)


def setup_inputs(seed: int = 0) -> dict:
    key_list = jax.random.split(jax.random.key(seed), 6)
    return {
        "electric": gaussian(key_list[0], (3, NZ, NX, NY), 1.0, 6.0, ((1, 16), (2, 8), (3, 2)), jnp.float32),
        "magnetic": gaussian(key_list[1], (3, NZ, NX, NY), 1.0, 6.0, ((1, 16), (2, 8), (3, 2)), jnp.float32),
        "aux_state": gaussian(key_list[2], (4, 2, PML, NX, NY), 1.0, 6.0, ((3, 8), (4, 2)), jnp.float32),
        "material": plant((jax.random.randint(key_list[3], (NX, NY), 0, 3) < 1).astype(jnp.int32), jax.random.fold_in(key_list[3], 1), 0, 1),
        "kerr_strength": jnp.clip(jnp.exp(jax.random.uniform(key_list[4], (2,), jnp.float32, math.log(0.1), math.log(1.0))), 0.1, 1.0),
    }


courant = 0.5
pml_rate = 3.0
eps_clad = 2.085
eps_core = 4.0


def decay_rates(layer):
    depth_front = (layer - jnp.arange(layer)).astype(jnp.float32) / layer
    depth_back = (jnp.arange(layer) + 1).astype(jnp.float32) / layer
    depth = jnp.stack([depth_front, depth_back])
    return jnp.exp(-pml_rate * depth ** 3)


def forward_open(values):
    return jnp.concatenate([values[1:], jnp.zeros_like(values[:1])], 0) - values


def backward_open(values):
    return values - jnp.concatenate([jnp.zeros_like(values[:1]), values[:-1]], 0)


def forward_loop(values, axis):
    return jnp.roll(values, -1, axis) - values


def backward_loop(values, axis):
    return values - jnp.roll(values, 1, axis)


def absorb(derivative, state_pair, rates):
    layer = state_pair.shape[1]
    total = derivative.shape[0]
    front = rates[0][:, None, None] * state_pair[0] + (rates[0] - 1.0)[:, None, None] * derivative[:layer]
    back = rates[1][:, None, None] * state_pair[1] + (rates[1] - 1.0)[:, None, None] * derivative[total - layer:]
    merged = jnp.concatenate([derivative[:layer] + front, derivative[layer:total - layer], derivative[total - layer:] + back], 0)
    return merged, jnp.stack([front, back])


def reference(electric, magnetic, aux_state, material, kerr_strength):
    rates = decay_rates(PML)
    core = material == 1
    eps_lin = jnp.where(core, eps_core, eps_clad)
    kerr_cell = jnp.where(core, kerr_strength[1], kerr_strength[0])
    elec_x, elec_y, elec_z = electric[0], electric[1], electric[2]
    magn_x, magn_y, magn_z = magnetic[0], magnetic[1], magnetic[2]
    aux_list = [aux_state[0], aux_state[1], aux_state[2], aux_state[3]]
    for step_index in range(STEPS):
        slope_y, aux_list[0] = absorb(forward_open(elec_y), aux_list[0], rates)
        slope_x, aux_list[1] = absorb(forward_open(elec_x), aux_list[1], rates)
        magn_x = magn_x - courant * (forward_loop(elec_z, 2) - slope_y)
        magn_y = magn_y - courant * (slope_x - forward_loop(elec_z, 1))
        magn_z = magn_z - courant * (forward_loop(elec_y, 1) - forward_loop(elec_x, 2))
        factor = courant / (eps_lin + kerr_cell * (elec_x * elec_x + elec_y * elec_y + elec_z * elec_z))
        slope_hy, aux_list[2] = absorb(backward_open(magn_y), aux_list[2], rates)
        slope_hx, aux_list[3] = absorb(backward_open(magn_x), aux_list[3], rates)
        new_x = elec_x + factor * (backward_loop(magn_z, 2) - slope_hy)
        new_y = elec_y + factor * (slope_hx - backward_loop(magn_z, 1))
        new_z = elec_z + factor * (backward_loop(magn_y, 1) - backward_loop(magn_x, 2))
        fields = jnp.stack([new_x, new_y, new_z, magn_x, magn_y, magn_z])
        fields = jnp.concatenate([fields[:, 1:], jnp.zeros_like(fields[:, :1])], 1)
        elec_x, elec_y, elec_z = fields[0], fields[1], fields[2]
        magn_x, magn_y, magn_z = fields[3], fields[4], fields[5]
    return jnp.stack([elec_x, elec_y, elec_z]), jnp.stack([magn_x, magn_y, magn_z])
```

```python
import functools

import jax
import jax.numpy as jnp
from jax import lax
from jax.experimental import pallas as pl
from jax.experimental.pallas import tpu as pltpu
from jax.sharding import PartitionSpec as P

PML = 8
STEPS = 4
HALO = 4
DEEP = 8
PLANES = 16
ROWS = 16
LANES = 128
TALL = ROWS + 2 * HALO
WIDE = 2 * LANES
FIELDS = 6
DEPTHS = (8, 8, 7, 7, 7, 7)
SENT = sum(DEPTHS)
OWN = FIELDS * PLANES
AUX = 4 * PML
MAT = OWN + AUX
TAKEN = MAT + 1
GROUPS = (TAKEN + 15) // 16
KEPT = 5

courant = 0.5
pml_rate = 3.0
eps_clad = 2.085
eps_core = 4.0

VMEM = pl.BlockSpec(memory_space=pltpu.VMEM)
SMEM = pl.BlockSpec(memory_space=pltpu.SMEM)
F32 = jnp.float32


def decay_rates(layer):
    depth_front = (layer - jnp.arange(layer)).astype(jnp.float32) / layer
    depth_back = (jnp.arange(layer) + 1).astype(jnp.float32) / layer
    depth = jnp.stack([depth_front, depth_back])
    return jnp.exp(-pml_rate * depth**3)


def sent_index(c, z):
    return sum(DEPTHS[:c]) + z


def call(body, out_shape, in_specs, scratch=(), **more):
    n_out = len(out_shape)
    more.setdefault("out_specs", [VMEM] * n_out)
    return pl.pallas_call(
        body,
        out_shape=[jax.ShapeDtypeStruct(s, F32) for s in out_shape],
        in_specs=in_specs,
        scratch_shapes=list(scratch),
        compiler_params=pltpu.CompilerParams(vmem_limit_bytes=40 * 1024 * 1024),
        **more,
    )


def pack_body(e, h, aux, mat, low, mid, high, zstrip, ystrip):
    lane = lax.broadcasted_iota(jnp.int32, (ROWS, LANES), 1) // 8

    def strip(tiles):
        out = jnp.zeros((ROWS, LANES), F32)
        for k, tile in enumerate(tiles):
            out = jnp.where(lane == k, pltpu.roll(tile, (8 * k + HALO) % LANES, 1), out)
        return out

    strips = []
    for c in range(FIELDS):
        src = e if c < 3 else h
        for z in range(DEPTHS[c]):
            plane = src[c % 3, z]
            at = sent_index(c, z)
            low[at] = plane[0:4]
            mid[at] = plane[4:12]
            high[at] = plane[12:16]
        made = strip([src[c % 3, z] for z in range(PLANES)])
        ystrip[c] = made
        strips.append(made)
    half = lane < 8
    for j in range(3):
        zstrip[j] = jnp.where(half, strips[2 * j], pltpu.roll(strips[2 * j + 1], 64, 1))
    for j in range(2):
        ystrip[FIELDS + j] = strip([aux[2 * j + k // PML, 0, k % PML] for k in range(16)])
    ystrip[FIELDS + 2] = strip([mat[...]])


def rows_body(e, h, aux, mat, ystrip, to_left, to_right):
    def put(at, tile):
        to_left[at] = tile[0:4]
        to_right[at] = tile[12:16]

    for c in range(FIELDS):
        src = e if c < 3 else h
        for z in range(PLANES):
            put(c * PLANES + z, src[c % 3, z])
    for a in range(4):
        for k in range(PML):
            put(OWN + a * PML + k, aux[a, 0, k])
    put(MAT, mat[...])
    for g in range(GROUPS):
        put(TAKEN + g, ystrip[g])


def forward(value, axis):
    return pltpu.roll(value, value.shape[axis] - 1, axis) - value


def backward(value, axis):
    return value - pltpu.roll(value, 1, axis)


def absorb(slope, state, index, k, rate):
    old = state[index, k]
    kept = rate * (slope + old)
    state[index, k] = kept - slope
    return kept


def magnetic_plane(f, p, layer=None):
    ex, ey, ez = f[0, p], f[1, p], f[2, p]
    slope_y = f[1, p + 1] - ey
    slope_x = f[0, p + 1] - ex
    if layer is not None:
        state, k, rate = layer
        slope_y = absorb(slope_y, state, 0, k, rate)
        slope_x = absorb(slope_x, state, 1, k, rate)
    hx = f[3, p] - courant * (forward(ez, 1) - slope_y)
    hy = f[4, p] - courant * (slope_x - forward(ez, 0))
    hz = f[5, p] - courant * (forward(ey, 0) - forward(ex, 1))
    f[3, p] = hx
    f[4, p] = hy
    f[5, p] = hz
    return ex, ey, ez, hx, hy, hz


def whole_plane(f, cell, p, layer=None):
    ex, ey, ez, hx, hy, hz = magnetic_plane(f, p, layer)
    factor = courant / (cell[0] + cell[1] * (ex * ex + ey * ey + ez * ez))
    slope_hy = hy - f[4, p - 1]
    slope_hx = hx - f[3, p - 1]
    if layer is not None:
        state, k, rate = layer
        slope_hy = absorb(slope_hy, state, 2, k, rate)
        slope_hx = absorb(slope_hx, state, 3, k, rate)
    f[0, p] = ex + factor * (backward(hz, 1) - slope_hy)
    f[1, p] = ey + factor * (slope_hx - backward(hz, 0))
    f[2, p] = ez + factor * (backward(hy, 0) - backward(hx, 1))


def loop(start, stop, body):
    lax.fori_loop(start, stop, lambda i, _: (body(i), 0)[1], 0)


def early_body(
    place, rates, kerr, e, h, aux, mat, ystrip, left, right,
    out_e, out_h, kept, cell, f, state,
):
    at_front = place[0] == 0
    at_back = place[0] == place[1] - 1

    def tall(own, above, below):
        return jnp.concatenate([above, own, below], 0)

    def stripe(g):
        return tall(ystrip[g], left[TAKEN + g], right[TAKEN + g])

    def fill(dst, own, at):
        dst[:, 0:LANES] = tall(own, left[at], right[at])

    for c in range(FIELDS):
        src = e if c < 3 else h
        packed = stripe(c)
        for z in range(PLANES):
            dst = f.at[c, z]
            fill(dst, src[c % 3, z], c * PLANES + z)
            dst[:, LANES:WIDE] = pltpu.roll(packed, (2 * LANES - 8 * z - HALO) % LANES, 1)

    packed = stripe(FIELDS + 2)
    flag_own = tall(mat[...], left[MAT], right[MAT])
    flag = jnp.concatenate([flag_own, pltpu.roll(packed, LANES - HALO, 1)], 1) == 1.0
    cell[0] = jnp.where(flag, eps_core, eps_clad)
    cell[1] = jnp.where(flag, kerr[1], kerr[0])

    @pl.when(at_front | at_back)
    def _():
        for j in range(2):
            packed = stripe(FIELDS + j)
            for k in range(16):
                a, z = 2 * j + k // PML, k % PML
                dst = state.at[a, z]
                fill(dst, aux[a, 0, z], OWN + a * PML + z)
                dst[:, LANES:WIDE] = pltpu.roll(packed, (2 * LANES - 8 * k - HALO) % LANES, 1)

    @pl.when(at_back)
    def _():
        for c in range(FIELDS):
            for z in range(STEPS):
                f[c, PLANES + z] = jnp.zeros((TALL, WIDE), F32)

    def step(s):
        last = jnp.where(at_back, PLANES - 2 + s, PLANES - 1 - s)
        layer_from = jnp.where(at_front, s, jnp.where(at_back, PLANES - PML + s - 1, last + 1))
        layer_to = jnp.where(at_front, s + PML - 1, last + 1)
        first = jnp.where(at_front, s - 1, PLANES - PML + s - 1)

        @pl.when(at_front)
        def _():
            magnetic_plane(f, s - 1, (state, 0, rates[0]))

        @pl.when(jnp.logical_not(at_front))
        def _():
            magnetic_plane(f, s - 1)

        def plain(p):
            whole_plane(f, cell, p)

        def layered(p):
            k = p - first
            whole_plane(f, cell, p, (state, k, rates[k]))

        loop(s, layer_from, plain)
        loop(layer_from, layer_to, layered)
        loop(layer_to, last + 1, plain)

    loop(1, STEPS + 1, step)

    def give(z):
        for c in range(3):
            out_e[c, z] = f[c, z + STEPS, HALO : HALO + ROWS, 0:LANES]
            out_h[c, z] = f[3 + c, z + STEPS, HALO : HALO + ROWS, 0:LANES]

    loop(0, PLANES // 2, give)

    @pl.when(at_back)
    def _():
        loop(PLANES // 2, PLANES, give)

    for c in range(FIELDS):
        for z in range(KEPT):
            kept[c, z] = f[c, PLANES - KEPT + z]


def late_body(
    place, kept, cell, low, mid, high, above, below, zs, zs_left, zs_right, old_e, old_h,
    out_e, out_h, f,
):
    at_back = place[0] == place[1] - 1
    base = PLANES - KEPT

    @pl.when(at_back)
    def _():
        out_e[...] = old_e[...]
        out_h[...] = old_h[...]

    @pl.when(jnp.logical_not(at_back))
    def _():
        for c in range(FIELDS):
            for z in range(KEPT):
                f[c, z] = kept[c, z]
            packed = jnp.concatenate([zs_left[c // 2, 12:16], zs[c // 2], zs_right[c // 2, 0:4]], 0)
            for z in range(DEPTHS[c]):
                at = sent_index(c, z)
                dst = f.at[c, KEPT + z]
                dst[:, 0:LANES] = jnp.concatenate(
                    [above[at], low[at], mid[at], high[at], below[at]], 0
                )
                k = (c % 2) * 8 + z
                dst[:, LANES:WIDE] = pltpu.roll(packed, (2 * LANES - 8 * k - HALO) % LANES, 1)

        def step(s):
            loop(PLANES - s - base, PLANES + DEEP - s - base, lambda p: whole_plane(f, cell, p))

        loop(1, STEPS + 1, step)

        def give(z):
            for c in range(3):
                at = z + PLANES // 2 + STEPS - base
                out_e[c, z] = f[c, at, HALO : HALO + ROWS, 0:LANES]
                out_h[c, z] = f[3 + c, at, HALO : HALO + ROWS, 0:LANES]

        loop(0, PLANES // 2, give)


def shards(electric, magnetic, aux_state, material, kerr_strength):
    n_gz, n_gx, n_gy = (lax.axis_size(a) for a in ("gz", "gx", "gy"))
    position = lax.axis_index("gz")
    place = jnp.stack([position, jnp.int32(n_gz)]).astype(jnp.int32)
    end = (position != 0).astype(jnp.int32)
    rates = lax.dynamic_index_in_dim(decay_rates(PML), end, 0, keepdims=False)
    aux = lax.dynamic_slice_in_dim(aux_state, end, 1, 1)
    mat = material.astype(F32)

    back = [(i, i - 1) for i in range(1, n_gz)]
    to_right = [(i, (i + 1) % n_gx) for i in range(n_gx)]
    to_left = [(i, (i - 1) % n_gx) for i in range(n_gx)]
    swap = [(i, (i + 1) % n_gy) for i in range(n_gy)]
    back_swap = [(i * n_gy + j, (i - 1) * n_gy + k) for i in range(1, n_gz) for j, k in swap]

    low, mid, high, zs, ys = call(
        pack_body,
        [(SENT, 4, LANES), (SENT, 8, LANES), (SENT, 4, LANES), (3, ROWS, LANES), (GROUPS, ROWS, LANES)],
        [VMEM] * 4,
    )(electric, magnetic, aux, mat)
    ys = lax.ppermute(ys, "gy", swap)
    low = lax.ppermute(low, "gz", back)
    high = lax.ppermute(high, "gz", back)
    zs = lax.ppermute(zs, ("gz", "gy"), back_swap)
    mid = lax.ppermute(mid, "gz", back)

    rows = (TAKEN + GROUPS, 4, LANES)
    my_first, my_last = call(rows_body, [rows, rows], [VMEM] * 5)(electric, magnetic, aux, mat, ys)
    from_left = lax.ppermute(my_last, "gx", to_right)
    from_right = lax.ppermute(my_first, "gx", to_left)

    part = (3, PLANES, ROWS, LANES)
    out_e, out_h, kept, cell = call(
        early_body,
        [part, part, (FIELDS, KEPT, TALL, WIDE), (2, TALL, WIDE)],
        [SMEM] * 3 + [VMEM] * 7,
        [
            pltpu.VMEM((FIELDS, PLANES + STEPS, TALL, WIDE), F32),
            pltpu.VMEM((4, PML, TALL, WIDE), F32),
        ],
        cost_estimate=pl.CostEstimate(flops=20_000_000, bytes_accessed=6_000_000, transcendentals=0),
    )(place, rates, kerr_strength, electric, magnetic, aux, mat, ys, from_left, from_right)

    above = lax.ppermute(high, "gx", to_right)
    below = lax.ppermute(low, "gx", to_left)
    zs_left = lax.ppermute(zs, "gx", to_right)
    zs_right = lax.ppermute(zs, "gx", to_left)

    half = pl.BlockSpec((3, PLANES // 2, ROWS, LANES), lambda i: (0, 1, 0, 0))

    out_e, out_h = call(
        late_body,
        [part, part],
        [SMEM] + [VMEM] * 10 + [half, half],
        [pltpu.VMEM((FIELDS, KEPT + DEEP, TALL, WIDE), F32)],
        grid=(1,),
        out_specs=[half, half],
        input_output_aliases={11: 0, 12: 1},
    )(place, kept, cell, low, mid, high, above, below, zs, zs_left, zs_right, out_e, out_h)
    return (out_e, out_h)


def solution(mesh):
    in_specs = (
        P(None, "gz", "gx", "gy"),
        P(None, "gz", "gx", "gy"),
        P(None, None, None, "gx", "gy"),
        P("gx", "gy"),
        P(),
    )
    out_specs = (P(None, "gz", "gx", "gy"), P(None, "gz", "gx", "gy"))
    return jax.shard_map(shards, mesh=mesh, in_specs=in_specs, out_specs=out_specs, check_vma=False)
```

```python
import math

import jax
import jax.numpy as jnp
from jax import lax
from jax.experimental import pallas as pl
from jax.experimental.pallas import tpu as pltpu
from jax.sharding import PartitionSpec as P

PML = 8
STEPS = 4
HALO = 4
DEEP = 8
PLANES = 16
ROWS = 16
LANES = 128
TALL = ROWS + 2 * HALO
WIDE = 2 * LANES
FIELDS = 6
DEPTHS = (8, 8, 7, 7, 7, 7)
SENT = sum(DEPTHS)
OWN = FIELDS * PLANES
AUX = 4 * PML
MAT = OWN + AUX
TAKEN = MAT + 1
GROUPS = (TAKEN + 15) // 16
KEPT = 5

courant = 0.5
pml_rate = 3.0
eps_clad = 2.085
eps_core = 4.0

VMEM = pl.BlockSpec(memory_space=pltpu.VMEM)
HBM = pl.BlockSpec(memory_space=pltpu.HBM)
F32 = jnp.float32


def front_rate(k):
    return math.exp(-pml_rate * ((PML - k) / PML) ** 3)


def back_rate(k):
    return math.exp(-pml_rate * ((k + 1) / PML) ** 3)


def ends():
    at = lax.axis_index("gz")
    return at == 0, at == lax.axis_size("gz") - 1


def sent_index(c, z):
    return sum(DEPTHS[:c]) + z


def call(body, out_shape, in_specs, scratch=(), **more):
    n_out = len(out_shape)
    more.setdefault("out_specs", [VMEM] * n_out)
    return pl.pallas_call(
        body,
        out_shape=[jax.ShapeDtypeStruct(s, F32) for s in out_shape],
        in_specs=in_specs,
        scratch_shapes=list(scratch),
        compiler_params=pltpu.CompilerParams(vmem_limit_bytes=40 * 1024 * 1024),
        cost_estimate=COST.get(body),
        **more,
    )


def strip(tiles):
    lane = lax.broadcasted_iota(jnp.int32, (ROWS, LANES), 1) // 8
    out = jnp.zeros((ROWS, LANES), F32)
    for k, tile in enumerate(tiles):
        out = jnp.where(lane == k, pltpu.roll(tile, (8 * k + HALO) % LANES, 1), out)
    return out


def unstrip(packed, k):
    return pltpu.roll(packed, (2 * LANES - 8 * k - HALO) % LANES, 1)


def deep_body(e, h, edge, mid, zstrip, token):
    for c in range(FIELDS):
        src = e if c < 3 else h
        for z in range(DEPTHS[c]):
            plane = src[c % 3, z]
            at = sent_index(c, z)
            edge[at] = plane[0:4]
            edge[SENT + at] = plane[12:16]
            mid[at] = plane[4:12]
        if c % 2:
            pair = [(c - 1, z) for z in range(DEEP)] + [(c, z) for z in range(DEEP)]
            zstrip[c // 2] = strip([(e if i < 3 else h)[i % 3, z] for i, z in pair])
    token[...] = jnp.zeros((8, LANES), F32)


def strip_body(e, h, aux, material, kerr, token, ystrip, chosen, mat, kerrs, sem):
    at_front, _ = ends()
    copy = pltpu.make_async_copy(aux.at[:, pl.ds(jnp.where(at_front, 0, 1), 1)], chosen, sem)
    copy.start()
    for c in range(FIELDS):
        src = e if c < 3 else h
        ystrip[c] = strip([src[c % 3, z] for z in range(PLANES)])
    mat[...] = material[...].astype(F32)
    ystrip[FIELDS + 2] = strip([mat[...]])
    for i in range(2):
        kerrs[i] = jnp.broadcast_to(kerr[0:1, i : i + 1], (8, LANES))
    copy.wait()
    for j in range(2):
        ystrip[FIELDS + j] = strip([chosen[2 * j + k // PML, 0, k % PML] for k in range(16)])


def tall(own, above, below):
    return jnp.concatenate([above, own, below], 0)


def relay_body(edge, zstrip, to_left, to_right):
    for at in range(SENT):
        to_left[at] = edge[at]
        to_right[at] = edge[SENT + at]
    for j in range(3):
        to_left[SENT + j] = zstrip[j, 0:4]
        to_right[SENT + j] = zstrip[j, 12:16]


def gather_body(edge, left, right, zstrip, cell, planes, strips):
    for at in range(SENT):
        planes[at, 0] = jnp.concatenate([left[at], edge[at]], 0)
        planes[at, 1] = jnp.concatenate([edge[SENT + at], right[at]], 0)
    for j in range(3):
        strips[j] = tall(zstrip[j], left[SENT + j], right[SENT + j])


def rows_body(e, h, aux, mat, ystrip, to_left, to_right):
    def put(at, tile):
        to_left[at] = tile[0:4]
        to_right[at] = tile[12:16]

    for c in range(FIELDS):
        src = e if c < 3 else h
        for z in range(PLANES):
            put(c * PLANES + z, src[c % 3, z])
    for a in range(4):
        for k in range(PML):
            put(OWN + a * PML + k, aux[a, 0, k])
    put(MAT, mat[...])
    for g in range(GROUPS):
        put(TAKEN + g, ystrip[g])


def forward(value, axis):
    return pltpu.roll(value, value.shape[axis] - 1, axis) - value


def backward(value, axis):
    return value - pltpu.roll(value, 1, axis)


def absorb(slope, state, index, k, rate):
    old = state[index, k]
    kept = rate * (slope + old)
    state[index, k] = kept - slope
    return kept


def magnetic_plane(read, write, p, layer=None):
    ex, ey, ez = (read(c, p) for c in range(3))
    slope_y = read(1, p + 1) - ey
    slope_x = read(0, p + 1) - ex
    if layer is not None:
        state, k, rate = layer
        slope_y = absorb(slope_y, state, 0, k, rate)
        slope_x = absorb(slope_x, state, 1, k, rate)
    write(3, p, read(3, p) - courant * (forward(ez, 1) - slope_y))
    write(4, p, read(4, p) - courant * (slope_x - forward(ez, 0)))
    write(5, p, read(5, p) - courant * (forward(ey, 0) - forward(ex, 1)))


def electric_plane(read, write, cell, p, layer=None):
    ex, ey, ez, hx, hy, hz = (read(c, p) for c in range(FIELDS))
    factor = courant / (cell[0] + cell[1] * (ex * ex + ey * ey + ez * ez))
    slope_hy = hy - read(4, p - 1)
    slope_hx = hx - read(3, p - 1)
    if layer is not None:
        state, k, rate = layer
        slope_hy = absorb(slope_hy, state, 2, k, rate)
        slope_hx = absorb(slope_hx, state, 3, k, rate)
    write(0, p, ex + factor * (backward(hz, 1) - slope_hy))
    write(1, p, ey + factor * (slope_hx - backward(hz, 0)))
    write(2, p, ez + factor * (backward(hy, 0) - backward(hx, 1)))


def inner(value):
    return value[HALO : HALO + ROWS, 0:LANES]


def early_body(
    kerr, e, h, aux, mat, ystrip, left, right,
    out_e, out_h, kept, cell, f, state, done, sems,
):
    at_front, at_back = ends()

    def stripe(g):
        return tall(ystrip[g], left[TAKEN + g], right[TAKEN + g])

    def fill(dst, own, at):
        dst[:, 0:LANES] = tall(own, left[at], right[at])

    for c in range(FIELDS):
        src = e if c < 3 else h
        packed = stripe(c)
        for z in range(PLANES):
            dst = f.at[c, z]
            fill(dst, src[c % 3, z], c * PLANES + z)
            dst[:, LANES:WIDE] = unstrip(packed, z)

    flag_own = tall(mat[...], left[MAT], right[MAT])
    flag = jnp.concatenate([flag_own, unstrip(stripe(FIELDS + 2), 0)], 1) == 1.0
    cell[0] = jnp.where(flag, eps_core, eps_clad)
    cell[1] = jnp.where(flag, kerr[1, 0:1, 0:1], kerr[0, 0:1, 0:1])

    @pl.when(at_front | at_back)
    def _():
        for j in range(2):
            packed = stripe(FIELDS + j)
            for k in range(16):
                a, z = 2 * j + k // PML, k % PML
                dst = state.at[a, z]
                fill(dst, aux[a, 0, z], OWN + a * PML + z)
                dst[:, LANES:WIDE] = unstrip(packed, k)

    @pl.when(at_back)
    def _():
        for c in range(FIELDS):
            for z in range(STEPS):
                f[c, PLANES + z] = jnp.zeros((TALL, WIDE), F32)

    def read(c, p):
        return f[c, p]

    def write(c, p, value):
        f[c, p] = value

    def run(last, layer_from, rate):
        for s in range(1, STEPS + 1):

            def layer(p):
                k = -1 if layer_from is None else p - layer_from(s)
                return (state, k, rate(k)) if 0 <= k < PML else None

            for p in range(s - 1, last(s) + 1):
                magnetic_plane(read, write, p, layer(p))
            for p in range(s, last(s) + 1):
                electric_plane(read, write, cell, p, layer(p))

    @pl.when(at_front)
    def _():
        run(lambda s: PLANES - 1 - s, lambda s: s - 1, front_rate)

    @pl.when(at_back)
    def _():
        run(lambda s: PLANES - 2 + s, lambda s: PLANES - PML + s - 1, back_rate)

    @pl.when(jnp.logical_not(at_front | at_back))
    def _():
        run(lambda s: PLANES - 1 - s, None, None)

    def send(at):
        span = pl.ds(at * PLANES // 2, PLANES // 2)
        for z in range(at * PLANES // 2, (at + 1) * PLANES // 2):
            for c in range(FIELDS):
                done[c, z] = inner(f[c, z + STEPS])
        copies = [
            pltpu.make_async_copy(done.at[pl.ds(3 * i, 3), span], out.at[:, span], sems.at[2 * at + i])
            for i, out in enumerate((out_e, out_h))
        ]
        for copy in copies:
            copy.start()
        return copies

    first = send(0)

    @pl.when(at_back)
    def _():
        for copy in send(1):
            copy.wait()

    for c in range(FIELDS):
        for z in range(KEPT):
            kept[c, z] = f[c, PLANES - KEPT + z]
    for copy in first:
        copy.wait()


def late_body(kept, cell, planes, strips, mid, old_e, old_h, out_e, out_h, f, done, sems):
    base = PLANES - KEPT
    span = pl.ds(PLANES // 2, PLANES // 2)

    @pl.when(jnp.logical_not(ends()[1]))
    def _():
        made = set()

        def read(c, p):
            if (c, p) in made:
                return f[c, p - base]
            if p < PLANES:
                return kept[c, p - base]
            at = sent_index(c, p - PLANES)
            own = jnp.concatenate([planes[at, 0], mid[at], planes[at, 1]], 0)
            side = unstrip(strips[c // 2], (c % 2) * DEEP + p - PLANES)
            return jnp.concatenate([own, side], 1)

        def write(c, p, value):
            if s == STEPS:
                done[c, p - PLANES // 2 - STEPS] = inner(value)
                if c >= 3:
                    f[c, p - base] = value
            else:
                f[c, p - base] = value
            made.add((c, p))

        def send(i):
            return pltpu.make_async_copy(
                done.at[pl.ds(3 * i, 3)], (out_e, out_h)[i].at[:, span], sems.at[i]
            )

        for s in range(1, STEPS + 1):
            window = range(PLANES - s, PLANES + DEEP - s)
            for p in window:
                magnetic_plane(read, write, p)
            if s == STEPS:
                send(1).start()
            for p in window:
                electric_plane(read, write, cell, p)
        send(0).start()
        send(1).wait()
        send(0).wait()


COST = {relay_body: pl.CostEstimate(flops=3_000_000_000, bytes_accessed=3_000_000_000, transcendentals=0)}


def shards(electric, magnetic, aux_state, material, kerr_strength):
    n_gz, n_gx, n_gy = (lax.axis_size(a) for a in ("gz", "gx", "gy"))
    back = [(i, i - 1) for i in range(1, n_gz)]
    to_right = [(i, (i + 1) % n_gx) for i in range(n_gx)]
    to_left = [(i, (i - 1) % n_gx) for i in range(n_gx)]
    swap = [(i, (i + 1) % n_gy) for i in range(n_gy)]
    back_swap = [(i * n_gy + j, (i - 1) * n_gy + k) for i in range(1, n_gz) for j, k in swap]
    dma = pltpu.SemaphoreType.DMA

    edge, mid, zs, token = call(
        deep_body,
        [(2 * SENT, 4, LANES), (SENT, 8, LANES), (3, ROWS, LANES), (8, LANES)],
        [VMEM, VMEM],
    )(electric[:, :DEEP], magnetic[:, :DEEP])
    edge = lax.ppermute(edge, "gz", back)
    zs = lax.ppermute(zs, ("gz", "gy"), back_swap)
    mid = lax.ppermute(mid, "gz", back)

    ys, aux, mat, kerr = call(
        strip_body,
        [(GROUPS, ROWS, LANES), (4, 1, PML, ROWS, LANES), (ROWS, LANES), (2, 8, LANES)],
        [VMEM, VMEM, HBM, VMEM, VMEM, VMEM],
        [dma(())],
    )(electric, magnetic, aux_state, material, kerr_strength[None], token)
    ys = lax.ppermute(ys, "gy", swap)

    rows = (TAKEN + GROUPS, 4, LANES)
    my_first, my_last = call(rows_body, [rows, rows], [VMEM] * 5)(electric, magnetic, aux, mat, ys)
    from_left = lax.ppermute(my_last, "gx", to_right)
    from_right = lax.ppermute(my_first, "gx", to_left)

    relayed = (SENT + 3, 4, LANES)
    go_left, go_right = call(
        relay_body, [relayed, relayed], [VMEM] * 2
    )(edge, zs)
    left = lax.ppermute(go_right, "gx", to_right)
    right = lax.ppermute(go_left, "gx", to_left)

    part = (3, PLANES, ROWS, LANES)
    out_e, out_h, kept, cell = call(
        early_body,
        [part, part, (FIELDS, KEPT, TALL, WIDE), (2, TALL, WIDE)],
        [VMEM] * 8,
        [
            pltpu.VMEM((FIELDS, PLANES + STEPS, TALL, WIDE), F32),
            pltpu.VMEM((4, PML, TALL, WIDE), F32),
            pltpu.VMEM((FIELDS, PLANES, ROWS, LANES), F32),
            dma((4,)),
        ],
        out_specs=[HBM, HBM, VMEM, VMEM],
    )(kerr, electric, magnetic, aux, mat, ys, from_left, from_right)

    planes, strips = call(
        gather_body, [(SENT, 2, 8, LANES), (3, TALL, LANES)], [VMEM] * 5
    )(edge, left, right, zs, cell)

    out_e, out_h = call(
        late_body,
        [part, part],
        [VMEM] * 5 + [HBM, HBM],
        [
            pltpu.VMEM((FIELDS, KEPT + DEEP, TALL, WIDE), F32),
            pltpu.VMEM((FIELDS, PLANES // 2, ROWS, LANES), F32),
            dma((2,)),
        ],
        out_specs=[HBM, HBM],
        input_output_aliases={5: 0, 6: 1},
    )(kept, cell, planes, strips, mid, out_e, out_h)
    return (out_e, out_h)


def solution(mesh):
    in_specs = (
        P(None, "gz", "gx", "gy"),
        P(None, "gz", "gx", "gy"),
        P(None, None, None, "gx", "gy"),
        P("gx", "gy"),
        P(),
    )
    out_specs = (P(None, "gz", "gx", "gy"), P(None, "gz", "gx", "gy"))
    return jax.shard_map(shards, mesh=mesh, in_specs=in_specs, out_specs=out_specs, check_vma=False)
```

```python
import math

import jax
import jax.numpy as jnp
from jax import lax
from jax.experimental import pallas as pl
from jax.experimental.pallas import tpu as pltpu
from jax.sharding import PartitionSpec as P

PML = 8
STEPS = 4
HALO = 4
DEEP = 8
PLANES = 16
ROWS = 16
LANES = 128
TALL = ROWS + 2 * HALO
WIDE = 2 * LANES
FIELDS = 6
DEPTHS = (8, 8, 7, 7, 7, 7)
SENT = sum(DEPTHS)
OWN = FIELDS * PLANES
AUX = 4 * PML
MAT = OWN + AUX
TAKEN = MAT + 1
GROUPS = (TAKEN + 15) // 16
KEPT = 5

courant = 0.5
pml_rate = 3.0
eps_clad = 2.085
eps_core = 4.0

VMEM = pl.BlockSpec(memory_space=pltpu.VMEM)
HBM = pl.BlockSpec(memory_space=pltpu.HBM)
F32 = jnp.float32


def front_rate(k):
    return math.exp(-pml_rate * ((PML - k) / PML) ** 3)


def back_rate(k):
    return math.exp(-pml_rate * ((k + 1) / PML) ** 3)


def ends():
    at = lax.axis_index("gz")
    return at == 0, at == lax.axis_size("gz") - 1


def sent_index(c, z):
    return sum(DEPTHS[:c]) + z


def call(body, out_shape, in_specs, scratch=(), **more):
    n_out = len(out_shape)
    more.setdefault("out_specs", [VMEM] * n_out)
    return pl.pallas_call(
        body,
        out_shape=[jax.ShapeDtypeStruct(s, F32) for s in out_shape],
        in_specs=in_specs,
        scratch_shapes=list(scratch),
        compiler_params=pltpu.CompilerParams(vmem_limit_bytes=40 * 1024 * 1024),
        cost_estimate=COST.get(body),
        **more,
    )


def strip(tiles):
    lane = lax.broadcasted_iota(jnp.int32, (ROWS, LANES), 1) // 8
    out = jnp.zeros((ROWS, LANES), F32)
    for k, tile in enumerate(tiles):
        out = jnp.where(lane == k, pltpu.roll(tile, (8 * k + HALO) % LANES, 1), out)
    return out


def unstrip(packed, k):
    return pltpu.roll(packed, (2 * LANES - 8 * k - HALO) % LANES, 1)


def deep_body(e, h, edge, mid, zstrip, token):
    for c in range(FIELDS):
        src = e if c < 3 else h
        for z in range(DEPTHS[c]):
            plane = src[c % 3, z]
            at = sent_index(c, z)
            edge[at] = plane[0:4]
            edge[SENT + at] = plane[12:16]
            mid[at] = plane[4:12]
        if c % 2:
            pair = [(c - 1, z) for z in range(DEEP)] + [(c, z) for z in range(DEEP)]
            zstrip[c // 2] = strip([(e if i < 3 else h)[i % 3, z] for i, z in pair])
    token[...] = jnp.zeros((8, LANES), F32)


def strip_body(e, h, aux, material, token, ystrip, chosen, mat, sem):
    at_front, _ = ends()
    copy = pltpu.make_async_copy(aux.at[:, pl.ds(jnp.where(at_front, 0, 1), 1)], chosen, sem)
    copy.start()
    for c in range(FIELDS):
        src = e if c < 3 else h
        ystrip[c] = strip([src[c % 3, z] for z in range(PLANES)])
    mat[...] = material[...].astype(F32)
    ystrip[FIELDS + 2] = strip([mat[...]])
    copy.wait()
    for j in range(2):
        ystrip[FIELDS + j] = strip([chosen[2 * j + k // PML, 0, k % PML] for k in range(16)])


def tall(own, above, below):
    return jnp.concatenate([above, own, below], 0)


def relay_body(edge, zstrip, to_left, to_right):
    for at in range(SENT):
        to_left[at] = edge[at]
        to_right[at] = edge[SENT + at]
    for j in range(3):
        to_left[SENT + j] = zstrip[j, 0:4]
        to_right[SENT + j] = zstrip[j, 12:16]


def gather_body(edge, left, right, zstrip, cell, planes, strips):
    for at in range(SENT):
        planes[at, 0] = jnp.concatenate([left[at], edge[at]], 0)
        planes[at, 1] = jnp.concatenate([edge[SENT + at], right[at]], 0)
    for j in range(3):
        strips[j] = tall(zstrip[j], left[SENT + j], right[SENT + j])


def rows_body(e, h, aux, mat, ystrip, kerr, to_left, to_right, kerrs):
    for i in range(2):
        kerrs[i] = jnp.broadcast_to(kerr[0:1, i : i + 1], (8, LANES))

    def put(at, tile):
        to_left[at] = tile[0:4]
        to_right[at] = tile[12:16]

    for c in range(FIELDS):
        src = e if c < 3 else h
        for z in range(PLANES):
            put(c * PLANES + z, src[c % 3, z])
    for a in range(4):
        for k in range(PML):
            put(OWN + a * PML + k, aux[a, 0, k])
    put(MAT, mat[...])
    for g in range(GROUPS):
        put(TAKEN + g, ystrip[g])


def forward(value, axis):
    return pltpu.roll(value, value.shape[axis] - 1, axis) - value


def backward(value, axis):
    return value - pltpu.roll(value, 1, axis)


def absorb(slope, state, index, k, rate):
    old = state[index, k]
    kept = rate * (slope + old)
    state[index, k] = kept - slope
    return kept


def magnetic_plane(read, write, p, layer=None):
    ex, ey, ez = (read(c, p) for c in range(3))
    slope_y = read(1, p + 1) - ey
    slope_x = read(0, p + 1) - ex
    if layer is not None:
        state, k, rate = layer
        slope_y = absorb(slope_y, state, 0, k, rate)
        slope_x = absorb(slope_x, state, 1, k, rate)
    write(3, p, read(3, p) - courant * (forward(ez, 1) - slope_y))
    write(4, p, read(4, p) - courant * (slope_x - forward(ez, 0)))
    write(5, p, read(5, p) - courant * (forward(ey, 0) - forward(ex, 1)))


def electric_plane(read, write, cell, p, layer=None):
    ex, ey, ez, hx, hy, hz = (read(c, p) for c in range(FIELDS))
    factor = courant / (cell[0] + cell[1] * (ex * ex + ey * ey + ez * ez))
    slope_hy = hy - read(4, p - 1)
    slope_hx = hx - read(3, p - 1)
    if layer is not None:
        state, k, rate = layer
        slope_hy = absorb(slope_hy, state, 2, k, rate)
        slope_hx = absorb(slope_hx, state, 3, k, rate)
    write(0, p, ex + factor * (backward(hz, 1) - slope_hy))
    write(1, p, ey + factor * (slope_hx - backward(hz, 0)))
    write(2, p, ez + factor * (backward(hy, 0) - backward(hx, 1)))


def inner(value):
    return value[HALO : HALO + ROWS, 0:LANES]


def early_body(
    kerr, e, h, aux, mat, ystrip, left, right,
    out_e, out_h, kept, cell, f, state, done, sems,
):
    at_front, at_back = ends()

    def stripe(g):
        return tall(ystrip[g], left[TAKEN + g], right[TAKEN + g])

    def fill(dst, own, at):
        dst[:, 0:LANES] = tall(own, left[at], right[at])

    for c in range(FIELDS):
        src = e if c < 3 else h
        packed = stripe(c)
        for z in range(PLANES):
            dst = f.at[c, z]
            fill(dst, src[c % 3, z], c * PLANES + z)
            dst[:, LANES:WIDE] = unstrip(packed, z)

    flag_own = tall(mat[...], left[MAT], right[MAT])
    flag = jnp.concatenate([flag_own, unstrip(stripe(FIELDS + 2), 0)], 1) == 1.0
    cell[0] = jnp.where(flag, eps_core, eps_clad)
    cell[1] = jnp.where(flag, kerr[1, 0:1, 0:1], kerr[0, 0:1, 0:1])

    @pl.when(at_front | at_back)
    def _():
        for j in range(2):
            packed = stripe(FIELDS + j)
            for k in range(16):
                a, z = 2 * j + k // PML, k % PML
                dst = state.at[a, z]
                fill(dst, aux[a, 0, z], OWN + a * PML + z)
                dst[:, LANES:WIDE] = unstrip(packed, k)

    @pl.when(at_back)
    def _():
        for c in range(FIELDS):
            for z in range(STEPS):
                f[c, PLANES + z] = jnp.zeros((TALL, WIDE), F32)

    def read(c, p):
        return f[c, p]

    def write(c, p, value):
        f[c, p] = value

    def run(last, layer_from, rate):
        for s in range(1, STEPS + 1):

            def layer(p):
                k = -1 if layer_from is None else p - layer_from(s)
                return (state, k, rate(k)) if 0 <= k < PML else None

            for p in range(s - 1, last(s) + 1):
                magnetic_plane(read, write, p, layer(p))
            for p in range(s, last(s) + 1):
                electric_plane(read, write, cell, p, layer(p))

    @pl.when(at_front)
    def _():
        run(lambda s: PLANES - 1 - s, lambda s: s - 1, front_rate)

    @pl.when(at_back)
    def _():
        run(lambda s: PLANES - 2 + s, lambda s: PLANES - PML + s - 1, back_rate)

    @pl.when(jnp.logical_not(at_front | at_back))
    def _():
        run(lambda s: PLANES - 1 - s, None, None)

    def send(at):
        span = pl.ds(at * PLANES // 2, PLANES // 2)
        for z in range(at * PLANES // 2, (at + 1) * PLANES // 2):
            for c in range(FIELDS):
                done[c, z] = inner(f[c, z + STEPS])
        copies = [
            pltpu.make_async_copy(done.at[pl.ds(3 * i, 3), span], out.at[:, span], sems.at[2 * at + i])
            for i, out in enumerate((out_e, out_h))
        ]
        for copy in copies:
            copy.start()
        return copies

    first = send(0)

    @pl.when(at_back)
    def _():
        for copy in send(1):
            copy.wait()

    for c in range(FIELDS):
        for z in range(KEPT):
            kept[c, z] = f[c, PLANES - KEPT + z]
    for copy in first:
        copy.wait()


def late_body(kept, cell, planes, strips, mid, old_e, old_h, out_e, out_h, f, done, sems):
    base = PLANES - KEPT
    span = pl.ds(PLANES // 2, PLANES // 2)

    @pl.when(jnp.logical_not(ends()[1]))
    def _():
        made = set()

        def read(c, p):
            if (c, p) in made:
                return f[c, p - base]
            if p < PLANES:
                return kept[c, p - base]
            at = sent_index(c, p - PLANES)
            own = jnp.concatenate([planes[at, 0], mid[at], planes[at, 1]], 0)
            side = unstrip(strips[c // 2], (c % 2) * DEEP + p - PLANES)
            return jnp.concatenate([own, side], 1)

        def write(c, p, value):
            if s == STEPS:
                done[c, p - PLANES // 2 - STEPS] = inner(value)
                if c >= 3:
                    f[c, p - base] = value
            else:
                f[c, p - base] = value
            made.add((c, p))

        def send(i):
            return pltpu.make_async_copy(
                done.at[pl.ds(3 * i, 3)], (out_e, out_h)[i].at[:, span], sems.at[i]
            )

        for s in range(1, STEPS + 1):
            window = range(PLANES - s, PLANES + DEEP - s)
            for p in window:
                magnetic_plane(read, write, p)
            if s == STEPS:
                send(1).start()
            for p in window:
                electric_plane(read, write, cell, p)
        send(0).start()
        send(1).wait()
        send(0).wait()


def cost(figure):
    return pl.CostEstimate(flops=figure, bytes_accessed=figure, transcendentals=0)


COST = {
    deep_body: cost(3_000_000_000),
    strip_body: cost(3_000_000_000),
    rows_body: cost(10_000_000_000),
    relay_body: cost(1_800_000_000),
}


def shards(electric, magnetic, aux_state, material, kerr_strength):
    n_gz, n_gx, n_gy = (lax.axis_size(a) for a in ("gz", "gx", "gy"))
    back = [(i, i - 1) for i in range(1, n_gz)]
    to_right = [(i, (i + 1) % n_gx) for i in range(n_gx)]
    to_left = [(i, (i - 1) % n_gx) for i in range(n_gx)]
    swap = [(i, (i + 1) % n_gy) for i in range(n_gy)]
    back_swap = [(i * n_gy + j, (i - 1) * n_gy + k) for i in range(1, n_gz) for j, k in swap]
    dma = pltpu.SemaphoreType.DMA

    edge, mid, zs, token = call(
        deep_body,
        [(2 * SENT, 4, LANES), (SENT, 8, LANES), (3, ROWS, LANES), (8, LANES)],
        [VMEM, VMEM],
    )(electric[:, :DEEP], magnetic[:, :DEEP])
    edge = lax.ppermute(edge, "gz", back)
    zs = lax.ppermute(zs, ("gz", "gy"), back_swap)
    mid = lax.ppermute(mid, "gz", back)

    ys, aux, mat = call(
        strip_body,
        [(GROUPS, ROWS, LANES), (4, 1, PML, ROWS, LANES), (ROWS, LANES)],
        [VMEM, VMEM, HBM, VMEM, VMEM],
        [dma(())],
    )(electric, magnetic, aux_state, material, token)
    ys = lax.ppermute(ys, "gy", swap)

    rows = (TAKEN + GROUPS, 4, LANES)
    my_first, my_last, kerr = call(rows_body, [rows, rows, (2, 8, LANES)], [VMEM] * 6)(
        electric, magnetic, aux, mat, ys, kerr_strength[None]
    )
    from_left = lax.ppermute(my_last, "gx", to_right)
    from_right = lax.ppermute(my_first, "gx", to_left)

    relayed = (SENT + 3, 4, LANES)
    go_left, go_right = call(
        relay_body, [relayed, relayed], [VMEM] * 2
    )(edge, zs)
    left = lax.ppermute(go_right, "gx", to_right)
    right = lax.ppermute(go_left, "gx", to_left)

    part = (3, PLANES, ROWS, LANES)
    out_e, out_h, kept, cell = call(
        early_body,
        [part, part, (FIELDS, KEPT, TALL, WIDE), (2, TALL, WIDE)],
        [VMEM] * 8,
        [
            pltpu.VMEM((FIELDS, PLANES + STEPS, TALL, WIDE), F32),
            pltpu.VMEM((4, PML, TALL, WIDE), F32),
            pltpu.VMEM((FIELDS, PLANES, ROWS, LANES), F32),
            dma((4,)),
        ],
        out_specs=[HBM, HBM, VMEM, VMEM],
    )(kerr, electric, magnetic, aux, mat, ys, from_left, from_right)

    planes, strips = call(
        gather_body, [(SENT, 2, 8, LANES), (3, TALL, LANES)], [VMEM] * 5
    )(edge, left, right, zs, cell)

    out_e, out_h = call(
        late_body,
        [part, part],
        [VMEM] * 5 + [HBM, HBM],
        [
            pltpu.VMEM((FIELDS, KEPT + DEEP, TALL, WIDE), F32),
            pltpu.VMEM((FIELDS, PLANES // 2, ROWS, LANES), F32),
            dma((2,)),
        ],
        out_specs=[HBM, HBM],
        input_output_aliases={5: 0, 6: 1},
    )(kept, cell, planes, strips, mid, out_e, out_h)
    return (out_e, out_h)


def solution(mesh):
    in_specs = (
        P(None, "gz", "gx", "gy"),
        P(None, "gz", "gx", "gy"),
        P(None, None, None, "gx", "gy"),
        P("gx", "gy"),
        P(),
    )
    out_specs = (P(None, "gz", "gx", "gy"), P(None, "gz", "gx", "gy"))
    return jax.shard_map(shards, mesh=mesh, in_specs=in_specs, out_specs=out_specs, check_vma=False)
```

```python
import math

import jax
import jax.numpy as jnp
from jax import lax
from jax.experimental import pallas as pl
from jax.experimental.pallas import tpu as pltpu
from jax.sharding import PartitionSpec as P

PML = 8
STEPS = 4
HALO = 4
DEEP = 8
PLANES = 16
ROWS = 16
LANES = 128
TALL = ROWS + 2 * HALO
WIDE = 2 * LANES
FIELDS = 6
DEPTHS = (8, 8, 7, 7, 7, 7)
SENT = sum(DEPTHS)
OWN = FIELDS * PLANES
AUX = 4 * PML
MAT = OWN + AUX
TAKEN = MAT + 1
GROUPS = (TAKEN + 15) // 16
KEPT = 5

courant = 0.5
pml_rate = 3.0
eps_clad = 2.085
eps_core = 4.0

VMEM = pl.BlockSpec(memory_space=pltpu.VMEM)
HBM = pl.BlockSpec(memory_space=pltpu.HBM)
F32 = jnp.float32


def front_rate(k):
    return math.exp(-pml_rate * ((PML - k) / PML) ** 3)


def back_rate(k):
    return math.exp(-pml_rate * ((k + 1) / PML) ** 3)


def ends():
    at = lax.axis_index("gz")
    return at == 0, at == lax.axis_size("gz") - 1


def sent_index(c, z):
    return sum(DEPTHS[:c]) + z


def call(body, out_shape, in_specs, scratch=(), **more):
    n_out = len(out_shape)
    more.setdefault("out_specs", [VMEM] * n_out)
    return pl.pallas_call(
        body,
        out_shape=[jax.ShapeDtypeStruct(s, F32) for s in out_shape],
        in_specs=in_specs,
        scratch_shapes=list(scratch),
        compiler_params=pltpu.CompilerParams(vmem_limit_bytes=40 * 1024 * 1024),
        cost_estimate=COST.get(body),
        **more,
    )


def strip(tiles):
    lane = lax.broadcasted_iota(jnp.int32, (ROWS, LANES), 1) // 8
    out = jnp.zeros((ROWS, LANES), F32)
    for k, tile in enumerate(tiles):
        out = jnp.where(lane == k, pltpu.roll(tile, (8 * k + HALO) % LANES, 1), out)
    return out


def unstrip(packed, k):
    return pltpu.roll(packed, (2 * LANES - 8 * k - HALO) % LANES, 1)


def deep_body(e, h, edge, mid, zstrip, token):
    for c in range(FIELDS):
        src = e if c < 3 else h
        for z in range(DEPTHS[c]):
            plane = src[c % 3, z]
            at = sent_index(c, z)
            edge[at] = plane[0:4]
            edge[SENT + at] = plane[12:16]
            mid[at] = plane[4:12]
        if c % 2:
            pair = [(c - 1, z) for z in range(DEEP)] + [(c, z) for z in range(DEEP)]
            zstrip[c // 2] = strip([(e if i < 3 else h)[i % 3, z] for i, z in pair])
    token[...] = jnp.zeros((8, LANES), F32)


def strip_body(e, h, aux, material, token, ystrip, chosen, mat, sem):
    at_front, _ = ends()
    copy = pltpu.make_async_copy(aux.at[:, pl.ds(jnp.where(at_front, 0, 1), 1)], chosen, sem)
    copy.start()
    for c in range(FIELDS):
        src = e if c < 3 else h
        ystrip[c] = strip([src[c % 3, z] for z in range(PLANES)])
    mat[...] = material[...].astype(F32)
    ystrip[FIELDS + 2] = strip([mat[...]])
    copy.wait()
    for j in range(2):
        ystrip[FIELDS + j] = strip([chosen[2 * j + k // PML, 0, k % PML] for k in range(16)])


def tall(own, above, below):
    return jnp.concatenate([above, own, below], 0)


def relay_body(edge, zstrip, kerr, to_left, to_right, kerrs):
    for i in range(2):
        kerrs[i] = jnp.broadcast_to(kerr[0:1, i : i + 1], (8, LANES))
    for at in range(SENT):
        to_left[at] = edge[at]
        to_right[at] = edge[SENT + at]
    for j in range(3):
        to_left[SENT + j] = zstrip[j, 0:4]
        to_right[SENT + j] = zstrip[j, 12:16]


def gather_body(edge, left, right, zstrip, cell, planes, strips):
    for at in range(SENT):
        planes[at, 0] = jnp.concatenate([left[at], edge[at]], 0)
        planes[at, 1] = jnp.concatenate([edge[SENT + at], right[at]], 0)
    for j in range(3):
        strips[j] = tall(zstrip[j], left[SENT + j], right[SENT + j])


def rows_body(e, h, aux, mat, ystrip, to_left, to_right):

    def put(at, tile):
        to_left[at] = tile[0:4]
        to_right[at] = tile[12:16]

    for c in range(FIELDS):
        src = e if c < 3 else h
        for z in range(PLANES):
            put(c * PLANES + z, src[c % 3, z])
    for a in range(4):
        for k in range(PML):
            put(OWN + a * PML + k, aux[a, 0, k])
    put(MAT, mat[...])
    for g in range(GROUPS):
        put(TAKEN + g, ystrip[g])


def forward(value, axis):
    return pltpu.roll(value, value.shape[axis] - 1, axis) - value


def backward(value, axis):
    return value - pltpu.roll(value, 1, axis)


def absorb(slope, state, index, k, rate):
    old = state[index, k]
    kept = rate * (slope + old)
    state[index, k] = kept - slope
    return kept


def magnetic_plane(read, write, p, layer=None):
    ex, ey, ez = (read(c, p) for c in range(3))
    slope_y = read(1, p + 1) - ey
    slope_x = read(0, p + 1) - ex
    if layer is not None:
        state, k, rate = layer
        slope_y = absorb(slope_y, state, 0, k, rate)
        slope_x = absorb(slope_x, state, 1, k, rate)
    write(3, p, read(3, p) - courant * (forward(ez, 1) - slope_y))
    write(4, p, read(4, p) - courant * (slope_x - forward(ez, 0)))
    write(5, p, read(5, p) - courant * (forward(ey, 0) - forward(ex, 1)))


def electric_plane(read, write, cell, p, layer=None):
    ex, ey, ez, hx, hy, hz = (read(c, p) for c in range(FIELDS))
    factor = courant / (cell[0] + cell[1] * (ex * ex + ey * ey + ez * ez))
    slope_hy = hy - read(4, p - 1)
    slope_hx = hx - read(3, p - 1)
    if layer is not None:
        state, k, rate = layer
        slope_hy = absorb(slope_hy, state, 2, k, rate)
        slope_hx = absorb(slope_hx, state, 3, k, rate)
    write(0, p, ex + factor * (backward(hz, 1) - slope_hy))
    write(1, p, ey + factor * (slope_hx - backward(hz, 0)))
    write(2, p, ez + factor * (backward(hy, 0) - backward(hx, 1)))


def inner(value):
    return value[HALO : HALO + ROWS, 0:LANES]


def early_body(
    kerr, e, h, aux, mat, ystrip, left, right,
    out_e, out_h, kept, cell, f, state, done, sems,
):
    at_front, at_back = ends()

    def stripe(g):
        return tall(ystrip[g], left[TAKEN + g], right[TAKEN + g])

    def fill(dst, own, at):
        dst[:, 0:LANES] = tall(own, left[at], right[at])

    for c in range(FIELDS):
        src = e if c < 3 else h
        packed = stripe(c)
        for z in range(PLANES):
            dst = f.at[c, z]
            fill(dst, src[c % 3, z], c * PLANES + z)
            dst[:, LANES:WIDE] = unstrip(packed, z)

    flag_own = tall(mat[...], left[MAT], right[MAT])
    flag = jnp.concatenate([flag_own, unstrip(stripe(FIELDS + 2), 0)], 1) == 1.0
    cell[0] = jnp.where(flag, eps_core, eps_clad)
    cell[1] = jnp.where(flag, kerr[1, 0:1, 0:1], kerr[0, 0:1, 0:1])

    @pl.when(at_front | at_back)
    def _():
        for j in range(2):
            packed = stripe(FIELDS + j)
            for k in range(16):
                a, z = 2 * j + k // PML, k % PML
                dst = state.at[a, z]
                fill(dst, aux[a, 0, z], OWN + a * PML + z)
                dst[:, LANES:WIDE] = unstrip(packed, k)

    @pl.when(at_back)
    def _():
        for c in range(FIELDS):
            for z in range(STEPS):
                f[c, PLANES + z] = jnp.zeros((TALL, WIDE), F32)

    def read(c, p):
        return f[c, p]

    def write(c, p, value):
        f[c, p] = value

    def run(last, layer_from, rate):
        for s in range(1, STEPS + 1):

            def layer(p):
                k = -1 if layer_from is None else p - layer_from(s)
                return (state, k, rate(k)) if 0 <= k < PML else None

            for p in range(s - 1, last(s) + 1):
                magnetic_plane(read, write, p, layer(p))
            for p in range(s, last(s) + 1):
                electric_plane(read, write, cell, p, layer(p))

    @pl.when(at_front)
    def _():
        run(lambda s: PLANES - 1 - s, lambda s: s - 1, front_rate)

    @pl.when(at_back)
    def _():
        run(lambda s: PLANES - 2 + s, lambda s: PLANES - PML + s - 1, back_rate)

    @pl.when(jnp.logical_not(at_front | at_back))
    def _():
        run(lambda s: PLANES - 1 - s, None, None)

    def send(at):
        span = pl.ds(at * PLANES // 2, PLANES // 2)
        for z in range(at * PLANES // 2, (at + 1) * PLANES // 2):
            for c in range(FIELDS):
                done[c, z] = inner(f[c, z + STEPS])
        copies = [
            pltpu.make_async_copy(done.at[pl.ds(3 * i, 3), span], out.at[:, span], sems.at[2 * at + i])
            for i, out in enumerate((out_e, out_h))
        ]
        for copy in copies:
            copy.start()
        return copies

    first = send(0)

    @pl.when(at_back)
    def _():
        for copy in send(1):
            copy.wait()

    for c in range(FIELDS):
        for z in range(KEPT):
            kept[c, z] = f[c, PLANES - KEPT + z]
    for copy in first:
        copy.wait()


def late_body(kept, cell, planes, strips, mid, old_e, old_h, out_e, out_h, f, done, sems):
    base = PLANES - KEPT
    span = pl.ds(PLANES // 2, PLANES // 2)

    @pl.when(jnp.logical_not(ends()[1]))
    def _():
        made = set()

        def read(c, p):
            if (c, p) in made:
                return f[c, p - base]
            if p < PLANES:
                return kept[c, p - base]
            at = sent_index(c, p - PLANES)
            own = jnp.concatenate([planes[at, 0], mid[at], planes[at, 1]], 0)
            side = unstrip(strips[c // 2], (c % 2) * DEEP + p - PLANES)
            return jnp.concatenate([own, side], 1)

        def write(c, p, value):
            if s == STEPS:
                done[c, p - PLANES // 2 - STEPS] = inner(value)
                if c >= 3:
                    f[c, p - base] = value
            else:
                f[c, p - base] = value
            made.add((c, p))

        def send(i):
            return pltpu.make_async_copy(
                done.at[pl.ds(3 * i, 3)], (out_e, out_h)[i].at[:, span], sems.at[i]
            )

        for s in range(1, STEPS + 1):
            window = range(PLANES - s, PLANES + DEEP - s)
            for p in window:
                magnetic_plane(read, write, p)
            if s == STEPS:
                send(1).start()
            for p in window:
                electric_plane(read, write, cell, p)
        send(0).start()
        send(1).wait()
        send(0).wait()


def cost(figure):
    return pl.CostEstimate(flops=figure, bytes_accessed=figure, transcendentals=0)


COST = {
    deep_body: cost(3_000_000_000),
    strip_body: cost(3_000_000_000),
    rows_body: cost(10_000_000_000),
    relay_body: cost(1_000_000_000),
}


def shards(electric, magnetic, aux_state, material, kerr_strength):
    n_gz, n_gx, n_gy = (lax.axis_size(a) for a in ("gz", "gx", "gy"))
    back = [(i, i - 1) for i in range(1, n_gz)]
    to_right = [(i, (i + 1) % n_gx) for i in range(n_gx)]
    to_left = [(i, (i - 1) % n_gx) for i in range(n_gx)]
    swap = [(i, (i + 1) % n_gy) for i in range(n_gy)]
    back_swap = [(i * n_gy + j, (i - 1) * n_gy + k) for i in range(1, n_gz) for j, k in swap]
    dma = pltpu.SemaphoreType.DMA

    edge, mid, zs, token = call(
        deep_body,
        [(2 * SENT, 4, LANES), (SENT, 8, LANES), (3, ROWS, LANES), (8, LANES)],
        [VMEM, VMEM],
    )(electric[:, :DEEP], magnetic[:, :DEEP])
    edge = lax.ppermute(edge, "gz", back)
    zs = lax.ppermute(zs, ("gz", "gy"), back_swap)
    mid = lax.ppermute(mid, "gz", back)

    ys, aux, mat = call(
        strip_body,
        [(GROUPS, ROWS, LANES), (4, 1, PML, ROWS, LANES), (ROWS, LANES)],
        [VMEM, VMEM, HBM, VMEM, VMEM],
        [dma(())],
    )(electric, magnetic, aux_state, material, token)
    ys = lax.ppermute(ys, "gy", swap)

    rows = (TAKEN + GROUPS, 4, LANES)
    my_first, my_last = call(rows_body, [rows, rows], [VMEM] * 5)(electric, magnetic, aux, mat, ys)
    from_left = lax.ppermute(my_last, "gx", to_right)
    from_right = lax.ppermute(my_first, "gx", to_left)

    relayed = (SENT + 3, 4, LANES)
    go_left, go_right, kerr = call(
        relay_body, [relayed, relayed, (2, 8, LANES)], [VMEM] * 3
    )(edge, zs, kerr_strength[None])
    left = lax.ppermute(go_right, "gx", to_right)
    right = lax.ppermute(go_left, "gx", to_left)

    part = (3, PLANES, ROWS, LANES)
    out_e, out_h, kept, cell = call(
        early_body,
        [part, part, (FIELDS, KEPT, TALL, WIDE), (2, TALL, WIDE)],
        [VMEM] * 8,
        [
            pltpu.VMEM((FIELDS, PLANES + STEPS, TALL, WIDE), F32),
            pltpu.VMEM((4, PML, TALL, WIDE), F32),
            pltpu.VMEM((FIELDS, PLANES, ROWS, LANES), F32),
            dma((4,)),
        ],
        out_specs=[HBM, HBM, VMEM, VMEM],
    )(kerr, electric, magnetic, aux, mat, ys, from_left, from_right)

    planes, strips = call(
        gather_body, [(SENT, 2, 8, LANES), (3, TALL, LANES)], [VMEM] * 5
    )(edge, left, right, zs, cell)

    out_e, out_h = call(
        late_body,
        [part, part],
        [VMEM] * 5 + [HBM, HBM],
        [
            pltpu.VMEM((FIELDS, KEPT + DEEP, TALL, WIDE), F32),
            pltpu.VMEM((FIELDS, PLANES // 2, ROWS, LANES), F32),
            dma((2,)),
        ],
        out_specs=[HBM, HBM],
        input_output_aliases={5: 0, 6: 1},
    )(kept, cell, planes, strips, mid, out_e, out_h)
    return (out_e, out_h)


def solution(mesh):
    in_specs = (
        P(None, "gz", "gx", "gy"),
        P(None, "gz", "gx", "gy"),
        P(None, None, None, "gx", "gy"),
        P("gx", "gy"),
        P(),
    )
    out_specs = (P(None, "gz", "gx", "gy"), P(None, "gz", "gx", "gy"))
    return jax.shard_map(shards, mesh=mesh, in_specs=in_specs, out_specs=out_specs, check_vma=False)
```

```python
import math

import jax
import jax.numpy as jnp
from jax import lax
from jax.experimental import pallas as pl
from jax.experimental.pallas import tpu as pltpu
from jax.sharding import PartitionSpec as P

PML = 8
STEPS = 4
HALO = 4
DEEP = 8
PLANES = 16
ROWS = 16
LANES = 128
TALL = ROWS + 2 * HALO
WIDE = 2 * LANES
FIELDS = 6
DEPTHS = (8, 8, 7, 7, 7, 7)
SENT = sum(DEPTHS)
OWN = FIELDS * PLANES
AUX = 4 * PML
MAT = OWN + AUX
TAKEN = MAT + 1
GROUPS = (TAKEN + 15) // 16
KEPT = 5

courant = 0.5
pml_rate = 3.0
eps_clad = 2.085
eps_core = 4.0

VMEM = pl.BlockSpec(memory_space=pltpu.VMEM)
HBM = pl.BlockSpec(memory_space=pltpu.HBM)
F32 = jnp.float32


def front_rate(k):
    return math.exp(-pml_rate * ((PML - k) / PML) ** 3)


def back_rate(k):
    return math.exp(-pml_rate * ((k + 1) / PML) ** 3)


def ends():
    at = lax.axis_index("gz")
    return at == 0, at == lax.axis_size("gz") - 1


def sent_index(c, z):
    return sum(DEPTHS[:c]) + z


def call(body, out_shape, in_specs, scratch=(), **more):
    n_out = len(out_shape)
    more.setdefault("out_specs", [VMEM] * n_out)
    return pl.pallas_call(
        body,
        out_shape=[jax.ShapeDtypeStruct(s, F32) for s in out_shape],
        in_specs=in_specs,
        scratch_shapes=list(scratch),
        compiler_params=pltpu.CompilerParams(vmem_limit_bytes=40 * 1024 * 1024),
        cost_estimate=COST.get(body),
        **more,
    )


def strip(tiles):
    lane = lax.broadcasted_iota(jnp.int32, (ROWS, LANES), 1) // 8
    out = jnp.zeros((ROWS, LANES), F32)
    for k, tile in enumerate(tiles):
        out = jnp.where(lane == k, pltpu.roll(tile, (8 * k + HALO) % LANES, 1), out)
    return out


def unstrip(packed, k):
    return pltpu.roll(packed, (2 * LANES - 8 * k - HALO) % LANES, 1)


def deep_body(e, h, edge, mid, zstrip, token):
    for c in range(FIELDS):
        src = e if c < 3 else h
        for z in range(DEPTHS[c]):
            plane = src[c % 3, z]
            at = sent_index(c, z)
            edge[at] = plane[0:4]
            edge[SENT + at] = plane[12:16]
            mid[at] = plane[4:12]
        if c % 2:
            pair = [(c - 1, z) for z in range(DEEP)] + [(c, z) for z in range(DEEP)]
            zstrip[c // 2] = strip([(e if i < 3 else h)[i % 3, z] for i, z in pair])
    token[...] = jnp.zeros((8, LANES), F32)


def strip_body(e, h, aux, material, token, ystrip, chosen, mat, sem):
    at_front, _ = ends()
    copy = pltpu.make_async_copy(aux.at[:, pl.ds(jnp.where(at_front, 0, 1), 1)], chosen, sem)
    copy.start()
    for c in range(FIELDS):
        src = e if c < 3 else h
        ystrip[c] = strip([src[c % 3, z] for z in range(PLANES)])
    mat[...] = material[...].astype(F32)
    ystrip[FIELDS + 2] = strip([mat[...]])
    copy.wait()
    for j in range(2):
        ystrip[FIELDS + j] = strip([chosen[2 * j + k // PML, 0, k % PML] for k in range(16)])


def tall(own, above, below):
    return jnp.concatenate([above, own, below], 0)


def relay_body(edge, zstrip, kerr, to_left, to_right, kerrs):
    for i in range(2):
        kerrs[i] = jnp.broadcast_to(kerr[0:1, i : i + 1], (8, LANES))
    for at in range(SENT):
        to_left[at] = edge[at]
        to_right[at] = edge[SENT + at]
    for j in range(3):
        to_left[SENT + j] = zstrip[j, 0:4]
        to_right[SENT + j] = zstrip[j, 12:16]


def gather_body(edge, left, right, zstrip, cell, planes, strips):
    for at in range(SENT):
        planes[at, 0] = jnp.concatenate([left[at], edge[at]], 0)
        planes[at, 1] = jnp.concatenate([edge[SENT + at], right[at]], 0)
    for j in range(3):
        strips[j] = tall(zstrip[j], left[SENT + j], right[SENT + j])


def rows_body(e, h, aux, mat, ystrip, to_left, to_right):

    def put(at, tile):
        to_left[at] = tile[0:4]
        to_right[at] = tile[12:16]

    for c in range(FIELDS):
        src = e if c < 3 else h
        for z in range(PLANES):
            put(c * PLANES + z, src[c % 3, z])
    for a in range(4):
        for k in range(PML):
            put(OWN + a * PML + k, aux[a, 0, k])
    put(MAT, mat[...])
    for g in range(GROUPS):
        put(TAKEN + g, ystrip[g])


def forward(value, axis):
    return pltpu.roll(value, value.shape[axis] - 1, axis) - value


def backward(value, axis):
    return value - pltpu.roll(value, 1, axis)


def absorb(slope, state, index, k, rate):
    old = state[index, k]
    kept = rate * (slope + old)
    state[index, k] = kept - slope
    return kept


def magnetic_plane(read, write, p, layer=None):
    ex, ey, ez = (read(c, p) for c in range(3))
    slope_y = read(1, p + 1) - ey
    slope_x = read(0, p + 1) - ex
    if layer is not None:
        state, k, rate = layer
        slope_y = absorb(slope_y, state, 0, k, rate)
        slope_x = absorb(slope_x, state, 1, k, rate)
    write(3, p, read(3, p) - courant * (forward(ez, 1) - slope_y))
    write(4, p, read(4, p) - courant * (slope_x - forward(ez, 0)))
    write(5, p, read(5, p) - courant * (forward(ey, 0) - forward(ex, 1)))


def electric_plane(read, write, cell, p, layer=None):
    ex, ey, ez, hx, hy, hz = (read(c, p) for c in range(FIELDS))
    factor = courant / (cell[0] + cell[1] * (ex * ex + ey * ey + ez * ez))
    slope_hy = hy - read(4, p - 1)
    slope_hx = hx - read(3, p - 1)
    if layer is not None:
        state, k, rate = layer
        slope_hy = absorb(slope_hy, state, 2, k, rate)
        slope_hx = absorb(slope_hx, state, 3, k, rate)
    write(0, p, ex + factor * (backward(hz, 1) - slope_hy))
    write(1, p, ey + factor * (slope_hx - backward(hz, 0)))
    write(2, p, ez + factor * (backward(hy, 0) - backward(hx, 1)))


def inner(value):
    return value[HALO : HALO + ROWS, 0:LANES]


def early_body(
    kerr, e, h, aux, mat, ystrip, left, right,
    out_e, out_h, kept, cell, f, state, done, sems,
):
    at_front, at_back = ends()

    def stripe(g):
        return tall(ystrip[g], left[TAKEN + g], right[TAKEN + g])

    def fill(dst, own, at):
        dst[:, 0:LANES] = tall(own, left[at], right[at])

    for c in range(FIELDS):
        src = e if c < 3 else h
        packed = stripe(c)
        for z in range(PLANES):
            dst = f.at[c, z]
            fill(dst, src[c % 3, z], c * PLANES + z)
            dst[:, LANES:WIDE] = unstrip(packed, z)

    flag_own = tall(mat[...], left[MAT], right[MAT])
    flag = jnp.concatenate([flag_own, unstrip(stripe(FIELDS + 2), 0)], 1) == 1.0
    cell[0] = jnp.where(flag, eps_core, eps_clad)
    cell[1] = jnp.where(flag, kerr[1, 0:1, 0:1], kerr[0, 0:1, 0:1])

    @pl.when(at_front | at_back)
    def _():
        for j in range(2):
            packed = stripe(FIELDS + j)
            for k in range(16):
                a, z = 2 * j + k // PML, k % PML
                dst = state.at[a, z]
                fill(dst, aux[a, 0, z], OWN + a * PML + z)
                dst[:, LANES:WIDE] = unstrip(packed, k)

    @pl.when(at_back)
    def _():
        for c in range(FIELDS):
            for z in range(STEPS):
                f[c, PLANES + z] = jnp.zeros((TALL, WIDE), F32)

    def read(c, p):
        return f[c, p]

    def write(c, p, value):
        f[c, p] = value

    def run(last, layer_from, rate):
        for s in range(1, STEPS + 1):

            def layer(p):
                k = -1 if layer_from is None else p - layer_from(s)
                return (state, k, rate(k)) if 0 <= k < PML else None

            for p in range(s - 1, last(s) + 1):
                magnetic_plane(read, write, p, layer(p))
            for p in range(s, last(s) + 1):
                electric_plane(read, write, cell, p, layer(p))

    @pl.when(at_front)
    def _():
        run(lambda s: PLANES - 1 - s, lambda s: s - 1, front_rate)

    @pl.when(at_back)
    def _():
        run(lambda s: PLANES - 2 + s, lambda s: PLANES - PML + s - 1, back_rate)

    @pl.when(jnp.logical_not(at_front | at_back))
    def _():
        run(lambda s: PLANES - 1 - s, None, None)

    def send(at):
        span = pl.ds(at * PLANES // 2, PLANES // 2)
        for z in range(at * PLANES // 2, (at + 1) * PLANES // 2):
            for c in range(FIELDS):
                done[c, z] = inner(f[c, z + STEPS])
        copies = [
            pltpu.make_async_copy(done.at[pl.ds(3 * i, 3), span], out.at[:, span], sems.at[2 * at + i])
            for i, out in enumerate((out_e, out_h))
        ]
        for copy in copies:
            copy.start()
        return copies

    first = send(0)

    @pl.when(at_back)
    def _():
        for copy in send(1):
            copy.wait()

    for c in range(FIELDS):
        for z in range(KEPT):
            kept[c, z] = f[c, PLANES - KEPT + z]
    for copy in first:
        copy.wait()


def late_body(kept, cell, planes, strips, mid, old_e, old_h, out_e, out_h, f, done, sems):
    base = PLANES - KEPT

    @pl.when(jnp.logical_not(ends()[1]))
    def _():
        made = set()

        def read(c, p):
            if (c, p) in made:
                return f[c, p - base]
            if p < PLANES:
                return kept[c, p - base]
            at = sent_index(c, p - PLANES)
            own = jnp.concatenate([planes[at, 0], mid[at], planes[at, 1]], 0)
            side = unstrip(strips[c // 2], (c % 2) * DEEP + p - PLANES)
            return jnp.concatenate([own, side], 1)

        def write(c, p, value):
            if s == STEPS:
                done[c, p - PLANES // 2 - STEPS] = inner(value)
                if c >= 3:
                    f[c, p - base] = value
            else:
                f[c, p - base] = value
            made.add((c, p))

        def send(i, part):
            size = PLANES // 4
            return pltpu.make_async_copy(
                done.at[pl.ds(3 * i, 3), pl.ds(part * size, size)],
                (out_e, out_h)[i].at[:, pl.ds(PLANES // 2 + part * size, size)],
                sems.at[2 * i + part],
            )

        for s in range(1, STEPS + 1):
            window = range(PLANES - s, PLANES + DEEP - s)
            for p in window:
                magnetic_plane(read, write, p)
            if s == STEPS:
                send(1, 0).start()
                send(1, 1).start()
            for p in window:
                electric_plane(read, write, cell, p)
                if s == STEPS and p == window[DEEP // 2 - 1]:
                    send(0, 0).start()
        send(0, 1).start()
        for i in (1, 0):
            for part in range(2):
                send(i, part).wait()


def cost(figure):
    return pl.CostEstimate(flops=figure, bytes_accessed=figure, transcendentals=0)


COST = {
    deep_body: cost(3_000_000_000),
    strip_body: cost(3_000_000_000),
    rows_body: cost(10_000_000_000),
    relay_body: cost(1_000_000_000),
}


def shards(electric, magnetic, aux_state, material, kerr_strength):
    n_gz, n_gx, n_gy = (lax.axis_size(a) for a in ("gz", "gx", "gy"))
    back = [(i, i - 1) for i in range(1, n_gz)]
    to_right = [(i, (i + 1) % n_gx) for i in range(n_gx)]
    to_left = [(i, (i - 1) % n_gx) for i in range(n_gx)]
    swap = [(i, (i + 1) % n_gy) for i in range(n_gy)]
    back_swap = [(i * n_gy + j, (i - 1) * n_gy + k) for i in range(1, n_gz) for j, k in swap]
    dma = pltpu.SemaphoreType.DMA

    edge, mid, zs, token = call(
        deep_body,
        [(2 * SENT, 4, LANES), (SENT, 8, LANES), (3, ROWS, LANES), (8, LANES)],
        [VMEM, VMEM],
    )(electric[:, :DEEP], magnetic[:, :DEEP])
    edge = lax.ppermute(edge, "gz", back)
    zs = lax.ppermute(zs, ("gz", "gy"), back_swap)
    mid = lax.ppermute(mid, "gz", back)

    ys, aux, mat = call(
        strip_body,
        [(GROUPS, ROWS, LANES), (4, 1, PML, ROWS, LANES), (ROWS, LANES)],
        [VMEM, VMEM, HBM, VMEM, VMEM],
        [dma(())],
    )(electric, magnetic, aux_state, material, token)
    ys = lax.ppermute(ys, "gy", swap)

    rows = (TAKEN + GROUPS, 4, LANES)
    my_first, my_last = call(rows_body, [rows, rows], [VMEM] * 5)(electric, magnetic, aux, mat, ys)
    from_left = lax.ppermute(my_last, "gx", to_right)
    from_right = lax.ppermute(my_first, "gx", to_left)

    relayed = (SENT + 3, 4, LANES)
    go_left, go_right, kerr = call(
        relay_body, [relayed, relayed, (2, 8, LANES)], [VMEM] * 3
    )(edge, zs, kerr_strength[None])
    left = lax.ppermute(go_right, "gx", to_right)
    right = lax.ppermute(go_left, "gx", to_left)

    part = (3, PLANES, ROWS, LANES)
    out_e, out_h, kept, cell = call(
        early_body,
        [part, part, (FIELDS, KEPT, TALL, WIDE), (2, TALL, WIDE)],
        [VMEM] * 8,
        [
            pltpu.VMEM((FIELDS, PLANES + STEPS, TALL, WIDE), F32),
            pltpu.VMEM((4, PML, TALL, WIDE), F32),
            pltpu.VMEM((FIELDS, PLANES, ROWS, LANES), F32),
            dma((4,)),
        ],
        out_specs=[HBM, HBM, VMEM, VMEM],
    )(kerr, electric, magnetic, aux, mat, ys, from_left, from_right)

    planes, strips = call(
        gather_body, [(SENT, 2, 8, LANES), (3, TALL, LANES)], [VMEM] * 5
    )(edge, left, right, zs, cell)

    out_e, out_h = call(
        late_body,
        [part, part],
        [VMEM] * 5 + [HBM, HBM],
        [
            pltpu.VMEM((FIELDS, KEPT + DEEP, TALL, WIDE), F32),
            pltpu.VMEM((FIELDS, PLANES // 2, ROWS, LANES), F32),
            dma((4,)),
        ],
        out_specs=[HBM, HBM],
        input_output_aliases={5: 0, 6: 1},
    )(kept, cell, planes, strips, mid, out_e, out_h)
    return (out_e, out_h)


def solution(mesh):
    in_specs = (
        P(None, "gz", "gx", "gy"),
        P(None, "gz", "gx", "gy"),
        P(None, None, None, "gx", "gy"),
        P("gx", "gy"),
        P(),
    )
    out_specs = (P(None, "gz", "gx", "gy"), P(None, "gz", "gx", "gy"))
    return jax.shard_map(shards, mesh=mesh, in_specs=in_specs, out_specs=out_specs, check_vma=False)
```
